1024 devices in a mesh: dp: 32 (over y, z_hi), tower: 32 (over z_lo, x, core).
Axes of the slice: x: 8, y: 8, z: 8 (z_hi: 4, z_lo: 2; z = z_hi * 2 + z_lo), core: 2. Of those that a mesh axis runs over, the one named last changes fastest.
Arguments:
- learner_image: bfloat16 [16384, 1152], P('dp')
- learner_text: bfloat16 [16384, 1152], P('dp')
- ref_image: bfloat16 [16384, 1152], P('dp')
- ref_text: bfloat16 [16384, 1152], P('dp')
- head_weight: bfloat16 [1152, 1152], P('tower'), may hold values from -0.1875 to 0.1875
- kept_index: int32 [8192], P('dp'), may hold values from 0 to 511, as said below
- kept_owner: int32 [8192, 1], P('dp'), may hold values from 0 to 31; in each aligned block of 256 rows (0 to 255, 256 to 511, ...) at most 32 rows name the same one
Outputs:
- learnability: float32 [16384], P(('dp', 'tower'))
- head_grad: float32 [1152, 1152], P('tower')
- owner_loss: float32 [32], P('dp')
The draws below stay inside these ranges and needn't reach their ends.
Inputs may be any that keep to these rules, and one draw needn't show every extreme that they name: `kept_index`: the 256 entries of one index of dp are distinct. `kept_owner`: among the 256 rows of one index of dp, no owner is named more than 32 times, a bound that some block reaches.
All inputs are finite; a program needn't handle non-finite values.
Results may differ from the reference program's by a relative error of at most 0.0029.
Values may be sent and summed in bfloat16 or wider, within the bound.
A program may use at most 32 MiB of HBM per device.

```python
import math
import jax
import jax.numpy as jnp
import numpy as np
from jax import lax

E = 1152
PAIRS_DEV = 512
KEEP_DEV = 256
CAP = 32
PAIRS = 16384
N_DP = 32


def embedding(key):
    key_normal = jax.random.fold_in(key, 0)
    key_scale = jax.random.fold_in(key, 3)
    entries = jax.random.normal(key_normal, (PAIRS, E), jnp.float32)
    row_scales = jnp.exp(jax.random.uniform(key_scale, (PAIRS, 1), jnp.float32, math.log(0.3), math.log(3.0)))
    return (entries * row_scales).astype(jnp.bfloat16)


def draw_learner_image(key, part):
    key = jax.random.fold_in(key, 11)
    return embedding(key)


def draw_learner_text(key, part):
    key = jax.random.fold_in(key, 12)
    return embedding(key)


def draw_ref_image(key, part):
    key = jax.random.fold_in(key, 13)
    return embedding(key)


def draw_ref_text(key, part):
    key = jax.random.fold_in(key, 14)
    return embedding(key)


def pick_block(block_key):
    return jax.random.permutation(block_key, PAIRS_DEV)[:KEEP_DEV]


def draw_kept_index(key, part):
    key = jax.random.fold_in(key, 21)
    dp_keys = jax.random.split(key, N_DP)
    chosen = jax.vmap(pick_block)(dp_keys)
    return chosen.reshape(-1).astype(jnp.int32)


def block_levels(rng, shape, cuts, least, top_value):
    factor_of, own = 1.0, jax.random.fold_in(rng, 6)
    for position, shards_of in cuts:
        heights = jnp.exp(jax.random.uniform(jax.random.fold_in(own, position), (shards_of,), jnp.float32, least / len(cuts), top_value / len(cuts)))
        factor_of = factor_of * jnp.repeat(heights, shape[position] // shards_of).reshape([-1 if axis == position else 1 for axis in range(len(shape))])
    return factor_of


def assign_block(own_key, own, number, rows, amount, top, limit, lean):
    sequence = jax.random.permutation(own_key, amount)
    packed, common = shares(amount, rows * top, limit, lean, True), shares(amount, rows * top, limit, lean, False)
    places = jnp.arange(amount)

    def named(sizes, turn):
        used = int((sizes > 0).sum())
        fixed = max(1, used // 4)
        shifted = fixed + (places - fixed + turn * (used - fixed)) % max(1, amount - fixed)
        return jnp.zeros((amount,), jnp.int32).at[sequence[jnp.where(places < fixed, places, shifted)]].set(jnp.asarray(sizes, jnp.int32))

    sizes = jnp.where(number % 4 == 0, named(packed, number // 4), named(common, number - number // 4 - 1))
    mixed = jax.random.permutation(jax.random.fold_in(own, 3), amount)
    giver, sink = mixed[0:amount // 2 * 2:2], mixed[1:amount // 2 * 2:2]
    slack = jnp.minimum(sizes[giver] - 1, limit - sizes[sink]) // 2
    slack = jnp.where((giver == sequence[0]) | (sink == sequence[0]) | (sizes[sink] == 0), 0, jnp.maximum(slack, 0))
    shifted = jax.random.randint(jax.random.fold_in(own, 4), (amount // 2,), 0, 1 << 20) % (slack + 1)
    sizes = sizes.at[giver].add(-shifted).at[sink].add(shifted)
    members = jnp.searchsorted(jnp.cumsum(sizes), jnp.arange(rows * top), side="right").astype(jnp.int32)
    grid = members.reshape(top, rows).T
    grid = grid[jax.random.permutation(jax.random.fold_in(own, 1), rows)]
    turn = jax.random.randint(jax.random.fold_in(own, 2), (rows, 1), 0, top)
    return jnp.take_along_axis(grid, (jnp.arange(top)[None, :] + turn) % top, axis=1)


def shares(number_of, total, limit, skew, full):
    weights = [(1 << 20) // math.isqrt(grade ** skew) + 1 for grade in range(1, number_of + 1)]
    largest = limit if full else min(limit, max(-(-total // number_of), total * weights[0] // sum(weights)))
    least = 1 if total - largest >= number_of - 1 else 0
    given, rest = [largest] + [least] * (number_of - 1), total - largest - least * (number_of - 1)
    while rest > 0:
        movable = [i for i in range(1, number_of) if given[i] < largest] or [i for i in range(1, number_of) if given[i] < limit]
        mass, left = sum([weights[i] for i in movable]), rest
        for i in movable:
            addition = min(limit - given[i], max(1, left * weights[i] // mass), rest)
            given[i] = given[i] + addition
            rest = rest - addition
    return np.array(given)


def bell_draw(stream_key, extent, spread, reach, pieces=(), kind=jnp.bfloat16):
    loudness = block_levels(stream_key, extent, pieces, -0.22, 0.18) if pieces else 1.0
    result = jax.random.normal(stream_key, extent, jnp.float32) * spread * loudness
    return jnp.minimum(jnp.maximum(result, -reach), reach).astype(kind)


def setup_inputs(seed: int = 0) -> dict:
    arg_keys = jax.random.split(jax.random.key(seed), 8)
    learner_image = draw_learner_image(jax.random.fold_in(arg_keys[7], 71), 0)
    learner_text = draw_learner_text(jax.random.fold_in(arg_keys[7], 71), 0)
    ref_image = draw_ref_image(jax.random.fold_in(arg_keys[7], 71), 0)
    ref_text = draw_ref_text(jax.random.fold_in(arg_keys[7], 71), 0)
    head_weight = bell_draw(arg_keys[4], (E, E), E ** -0.5, 0.1875, ((0, 32),))
    kept_index = draw_kept_index(jax.random.fold_in(arg_keys[7], 71), 0)
    kept_owner_keys = jax.random.split(jax.random.fold_in(arg_keys[6], 1), (N_DP * KEEP_DEV) // KEEP_DEV)
    kept_owner_turns = jax.random.permutation(jax.random.fold_in(arg_keys[6], 3), (N_DP * KEEP_DEV) // KEEP_DEV)
    kept_owner = jax.vmap(lambda own, number: assign_block(jax.random.fold_in(arg_keys[6], 2), own, number, KEEP_DEV, N_DP, 1, CAP, 2))(kept_owner_keys, kept_owner_turns).reshape((N_DP * KEEP_DEV, 1))
    return dict(learner_image=learner_image, learner_text=learner_text, ref_image=ref_image, ref_text=ref_text, head_weight=head_weight, kept_index=kept_index, kept_owner=kept_owner)


def row_losses(image, text):
    logit_scale = 1.0 / math.sqrt(E)
    column_ids = jnp.arange(PAIRS, dtype=jnp.int32)

    def one_block(block):
        block_rows, first_row = block
        logits = jnp.dot(block_rows, text.T, preferred_element_type=jnp.float32) * logit_scale
        row_ids = first_row + jnp.arange(PAIRS_DEV, dtype=jnp.int32)
        positive = row_ids[:, None] == column_ids[None, :]
        pair_terms = jnp.where(positive, jax.nn.softplus(-logits), jax.nn.softplus(logits) / PAIRS_DEV)
        return lax.optimization_barrier(jnp.sum(pair_terms, 1))
    starts = jnp.arange(N_DP, dtype=jnp.int32) * PAIRS_DEV
    totals = lax.map(one_block, (image.reshape(N_DP, PAIRS_DEV, E), starts))
    return totals.reshape(PAIRS)

def reference(learner_image, learner_text, ref_image, ref_text, head_weight, kept_index, kept_owner):
    learnability = row_losses(learner_image, learner_text) - row_losses(ref_image, ref_text)
    offsets = (jnp.arange(N_DP, dtype=jnp.int32) * PAIRS_DEV)[:, None]
    chosen = (offsets + kept_index.reshape(N_DP, KEEP_DEV).astype(jnp.int32)).reshape(-1)
    kept_image = learner_image[chosen]
    kept_text = learner_text[chosen]
    projected = jnp.dot(kept_image, head_weight.T, preferred_element_type=jnp.float32)
    head_logit = lax.optimization_barrier(jnp.sum(projected * kept_text.astype(jnp.float32), 1)) / math.sqrt(E)
    head_loss = jax.nn.softplus(-head_logit)
    head_slope = -jax.nn.sigmoid(-head_logit) / math.sqrt(E)
    slope_text = (head_slope[:, None] * kept_text.astype(jnp.float32)).astype(jnp.bfloat16)
    head_grad = jnp.dot(slope_text.T, kept_image, preferred_element_type=jnp.float32)
    owners = jnp.arange(N_DP, dtype=jnp.int32)
    owner_table = (kept_owner[:, 0][:, None] == owners[None, :]).astype(jnp.float32)
    owner_loss = lax.optimization_barrier(jnp.sum(owner_table * head_loss[:, None], 0))
    return (learnability, head_grad, owner_loss)
```

```python
import math

import jax
import jax.numpy as jnp
from jax import lax
from jax.experimental import pallas as pl
from jax.experimental.pallas import tpu as pltpu
from jax.sharding import PartitionSpec as P

MESH = pl.DeviceIdType.MESH
N_Y, N_ZH, N_ZL, N_X, N_C = 8, 4, 2, 8, 2
POS = (0, 2, 4, 6, 7, 5, 3, 1)
TILES = 6
LOG2E = 1.4426950408889634


def kernel(li, lt, ri, rt, w, ki, ko, learn, grad, owner,
           img, txt, wv, kiv, kov, buf, tz, tx, tsrc, lz, lx, lsrc,
           chunks, rsbuf, red, zbuf, agbuf, ls, ss, rs):
    pairs, width = img.shape[1], img.shape[2]
    cols = w.shape[0]
    piece = pairs // (N_ZL * N_X * N_C)
    block = piece * N_ZH
    scale = 1.0 / math.sqrt(width)
    d, t = lax.axis_index("dp"), lax.axis_index("tower")
    y, zh = d // N_ZH, d % N_ZH
    q, x = (t // (N_X * N_C)) * N_C + t % N_C, (t // N_C) % N_X

    def at_y(k):
        return (((y + k) % N_Y) * N_ZH + zh, t)

    def at_z(k):
        return (y * N_ZH + (zh + k) % N_ZH, t)

    def at_q(k):
        r = (q + k) % (N_ZL * N_C)
        return (d, (r // N_C) * (N_X * N_C) + x * N_C + r % N_C)

    def at_x(k):
        return (d, (q // N_C) * (N_X * N_C) + ((x + k) % N_X) * N_C + q % N_C)

    peers = [at_y(k) for k in range(1, N_Y)] + [at_z(k) for k in range(1, N_ZH)]
    peers += [at_q(k) for k in range(1, N_ZL * N_C)] + [at_x(k) for k in range(1, N_X)]
    sent = []

    def send(src, dst, device):
        i = len(sent)
        copy = pltpu.make_async_remote_copy(
            src_ref=src, dst_ref=dst, send_sem=ss.at[i], recv_sem=rs.at[i],
            device_id=device, device_id_type=MESH)
        copy.start()
        sent.append(copy)
        return copy

    barrier = pltpu.get_barrier_semaphore()
    for p in peers:
        pl.semaphore_signal(barrier, inc=1, device_id=p, device_id_type=MESH)
    own = pl.ds(pl.multiple_of(t * piece, piece), piece)
    loads = [(lt.at[own], buf.at[0, pl.ds(0, piece)]), (rt.at[own], buf.at[1, pl.ds(0, piece)]),
             (li, img.at[0]), (w, wv), (lt, txt), (ki, kiv), (ko, kov), (ri, img.at[1])]
    loads = [pltpu.make_async_copy(a, b, ls.at[i]) for i, (a, b) in enumerate(loads)]
    for c in loads:
        c.start()
    pl.semaphore_wait(barrier, len(peers))

    def rows(r, z, n):
        return pl.ds(POS[r % N_Y] * block + z * piece, n)

    z_in = {}
    y_in = {}
    texts = (lt, rt)
    for m in range(2):
        for k in (1, 3):
            z_in[m, k] = send(texts[m].at[own], buf.at[m, rows(0, N_ZH - k, piece)], at_z(k))
        for s in (1, -1):
            y_in[m, s, 0] = [send(texts[m].at[own], buf.at[m, rows(-s, 0, piece)], at_y(s))]
    for m in range(2):
        z_in[m, 2] = send(texts[m].at[own], buf.at[m, rows(0, 2, piece)], at_z(2))

    for c in loads[:5]:
        c.wait()
    nt = (((1,), (1,)), ((), ()))

    def dot_nt(a, b):
        return lax.dot_general(a, b, nt, preferred_element_type=jnp.float32)

    pad = -(-cols // 8) * 8
    col = lax.broadcasted_iota(jnp.int32, (pad, width), 0)
    place = lax.broadcasted_iota(jnp.int32, (pad, width), 1)
    choose = jnp.where((place == t * cols + col) & (col < cols), 1.0, 0.0).astype(jnp.bfloat16)
    text_cols = dot_nt(choose, txt[...])
    projected = dot_nt(wv[...], img[0])
    part = jnp.sum(projected * text_cols[:cols], 0, keepdims=True)

    def tower_sum(value, src, first, second):
        src[0] = value
        first[q] = value
        got = [send(src.at[0], first.at[q], at_q(k)) for k in range(1, N_ZL * N_C)]

        def middle():
            for c in got:
                c.wait_recv()
            value = first[0]
            for k in range(1, N_ZL * N_C):
                value = value + first[k]
            src[1] = value
            second[x] = value
            got2 = [send(src.at[1], second.at[x], at_x(k)) for k in range(1, N_X)]

            def last():
                for c in got2:
                    c.wait_recv()
                value = second[0]
                for k in range(1, N_X):
                    value = value + second[k]
                return value
            return last
        return middle

    head_middle = tower_sum(part, tsrc, tz, tx)

    for k in (1, 3, 2):
        for m in range(2):
            z_in[m, k].wait_recv()
            for s in (1, -1):
                y_in[m, s, 0].append(
                    send(buf.at[m, rows(0, N_ZH - k, piece)],
                         buf.at[m, rows(-s, N_ZH - k, piece)], at_y(s)))

    for c in loads[5:]:
        c.wait()

    lane = lax.broadcasted_iota(jnp.int32, (8, pairs), 1)
    sub = lax.broadcasted_iota(jnp.int32, (8, pairs), 0)

    def losses(m, start, count, with_own):
        logits = dot_nt(buf[m, start:start + count], img[m])
        linear = jnp.zeros((8, pairs), jnp.float32)
        prod = jnp.zeros((8, pairs), jnp.float32)
        diag = jnp.zeros((8, pairs), jnp.float32)
        for g in range(count // 8):
            v = logits[8 * g:8 * g + 8]
            e = jnp.exp2(-jnp.abs(v * (scale * LOG2E)))
            lin = jnp.maximum(v * (scale / pairs), 0.0)
            if with_own and g < piece // 8:
                is_diag = lane == t * piece + 8 * g + sub
                diag = diag + jnp.where(is_diag, jnp.maximum(-v * scale, 0.0) + jnp.log1p(e), 0.0)
                e = jnp.where(is_diag, 0.0, e)
                lin = jnp.where(is_diag, 0.0, lin)
            linear = linear + lin
            prod = prod * (1.0 + e) + e
        return diag + linear + jnp.log1p(prod) * (1.0 / pairs)

    def both(start, count, with_own=False):
        return losses(0, start, count, with_own) - losses(1, start, count, with_own)

    total = both(0, block, True)

    head_last = head_middle()

    def relay(step):
        for m in range(2):
            for s in (1, -1):
                if (m, s, step) in y_in:
                    for c in y_in[m, s, step]:
                        c.wait_recv()
                    r = -s * (step + 1)
                    if step < 2 or (step == 2 and (s == 1) == (m == 0)):
                        y_in[m, s, step + 1] = [
                            send(buf.at[m, rows(r, 0, block)], buf.at[m, rows(r - s, 0, block)], at_y(s))]

    relay(0)
    total = total + both(block, 2 * block)

    head_logit = head_last() * scale
    e = jnp.exp(-jnp.abs(head_logit))
    head_loss = jnp.maximum(-head_logit, 0.0) + jnp.log1p(e)
    slope = -(jnp.where(head_logit >= 0.0, e, 1.0) / (1.0 + e)) * scale
    kept = kiv.shape[1]
    hit = lax.broadcasted_iota(jnp.int32, (pairs, kept), 0) == kiv[...]
    hit = jnp.where(hit, 1.0, 0.0).astype(jnp.bfloat16)
    owner_plus = jnp.broadcast_to(kov[...].astype(jnp.float32) + 1.0, (16, kept)).astype(jnp.bfloat16)
    owner_of = dot_nt(owner_plus, hit)[:1]
    slope = jnp.where(owner_of > 0.5, slope, 0.0)
    slope_text = (text_cols * slope).astype(jnp.bfloat16)
    grad_part = jnp.dot(slope_text, img[0], preferred_element_type=jnp.float32)
    n_dp = N_Y * N_ZH
    each = lax.broadcasted_iota(jnp.int32, (n_dp, pairs), 0)
    mine = owner_of == (each + 1).astype(jnp.float32)
    owner_col = jnp.sum(jnp.where(mine, head_loss, 0.0), 1, keepdims=True)
    on_lane = lax.broadcasted_iota(jnp.int32, (n_dp, 128), 0) == lax.broadcasted_iota(jnp.int32, (n_dp, 128), 1)
    owner_row = jnp.sum(jnp.where(on_lane, owner_col, 0.0), 0, keepdims=True)
    wide = width // 128
    n_tiles = (pad // 8) * wide
    for i in range(N_Y * TILES):
        if i < n_tiles:
            a, b = 8 * (i // wide), 128 * (i % wide)
            tile = grad_part[a:a + 8, b:b + 128]
        elif i == n_tiles:
            tile = jnp.broadcast_to(owner_row, (8, 128))
        else:
            tile = jnp.zeros((8, 128), jnp.float32)
        chunks[i // TILES, i % TILES] = tile
    got = [send(chunks.at[(y + k) % N_Y], rsbuf.at[k - 1], at_y(k)) for k in range(1, N_Y)]

    relay(1)
    total = total + both(3 * block, 2 * block)

    for c in got:
        c.wait_recv()
    value = chunks[y]
    for k in range(N_Y - 1):
        value = value + rsbuf[k]
    red[...] = value
    zbuf[zh] = value
    got = [send(red, zbuf.at[zh], at_z(k)) for k in range(1, N_ZH)]

    relay(2)
    total = total + both(5 * block, 2 * block)

    for c in got:
        c.wait_recv()
    value = zbuf[0]
    for k in range(1, N_ZH):
        value = value + zbuf[k]
    agbuf[y] = value
    got = [send(agbuf.at[y], agbuf.at[y], at_y(k)) for k in range(1, N_Y)]

    relay(3)
    total = total + both(7 * block, block)
    learn_middle = tower_sum(jnp.sum(total, 0, keepdims=True), lsrc, lz, lx)

    for c in got:
        c.wait_recv()
    for i in range(n_tiles):
        a, b = 8 * (i // wide), 128 * (i % wide)
        n = min(8, cols - a)
        grad[a:a + n, b:b + 128] = agbuf[i // TILES, i % TILES][:n]
    all_owners = agbuf[n_tiles // TILES, n_tiles % TILES][:1]
    pick = lax.broadcasted_iota(jnp.int32, (1, 128), 1) == d
    owner[...] = jnp.broadcast_to(jnp.sum(jnp.where(pick, all_owners, 0.0), 1, keepdims=True), (1, 128))

    learn_last = learn_middle()
    diff = learn_last()
    moved = pltpu.roll(jnp.broadcast_to(diff, (8, pairs)), (pairs - t * piece) % pairs, 1)
    learn[...] = moved[:1, :128]
    for c in sent:
        c.wait_send()


def local(learner_image, learner_text, ref_image, ref_text, head_weight, kept_index, kept_owner):
    pairs, width = learner_image.shape
    cols = head_weight.shape[0]
    kept = kept_index.shape[0]
    f32, bf16, i32 = jnp.float32, jnp.bfloat16, jnp.int32
    any_space = pl.BlockSpec(memory_space=pl.ANY)
    vmem = pl.BlockSpec(memory_space=pltpu.VMEM)
    learn, grad, owner = pl.pallas_call(
        kernel,
        out_shape=(
            jax.ShapeDtypeStruct((1, 128), f32),
            jax.ShapeDtypeStruct((cols, width), f32),
            jax.ShapeDtypeStruct((1, 128), f32),
        ),
        in_specs=[any_space] * 7,
        out_specs=(vmem, vmem, vmem),
        scratch_shapes=[
            pltpu.VMEM((2, pairs, width), bf16),
            pltpu.VMEM((pairs, width), bf16),
            pltpu.VMEM((cols, width), bf16),
            pltpu.VMEM((1, kept), i32),
            pltpu.VMEM((1, kept), i32),
            pltpu.VMEM((2, pairs, width), bf16),
            pltpu.VMEM((4, 1, pairs), f32),
            pltpu.VMEM((8, 1, pairs), f32),
            pltpu.VMEM((2, 1, pairs), f32),
            pltpu.VMEM((4, 1, pairs), f32),
            pltpu.VMEM((8, 1, pairs), f32),
            pltpu.VMEM((2, 1, pairs), f32),
            pltpu.VMEM((N_Y, TILES, 8, 128), f32),
            pltpu.VMEM((N_Y - 1, TILES, 8, 128), f32),
            pltpu.VMEM((TILES, 8, 128), f32),
            pltpu.VMEM((N_ZH, TILES, 8, 128), f32),
            pltpu.VMEM((N_Y, TILES, 8, 128), f32),
            pltpu.SemaphoreType.DMA((8,)),
            pltpu.SemaphoreType.DMA((96,)),
            pltpu.SemaphoreType.DMA((96,)),
        ],
        compiler_params=pltpu.CompilerParams(
            collective_id=0, has_side_effects=True, vmem_limit_bytes=40 * 1024 * 1024
        ),
    )(
        learner_image,
        learner_text,
        ref_image,
        ref_text,
        head_weight,
        kept_index.reshape(1, kept),
        kept_owner.reshape(1, kept),
    )
    return learn[0, : pairs // 32], grad, owner[0, :1]


def solution(mesh):
    placed = (
        P("dp", None),
        P("dp", None),
        P("dp", None),
        P("dp", None),
        P("tower", None),
        P("dp"),
        P("dp", None),
    )
    return jax.shard_map(
        local,
        mesh=mesh,
        in_specs=placed,
        out_specs=(P(("dp", "tower")), P("tower", None), P("dp")),
        check_vma=False,
    )
```

```python
import math

import jax
import jax.numpy as jnp
from jax import lax
from jax.experimental import pallas as pl
from jax.experimental.pallas import tpu as pltpu
from jax.sharding import PartitionSpec as P

MESH = pl.DeviceIdType.MESH
N_Y, N_ZH, N_ZL, N_X, N_C = 8, 4, 2, 8, 2
POS = (0, 2, 4, 6, 7, 5, 3, 1)
ZPOS = (0, 1, 3, 2)
TILES = 6
LOG2E = 1.4426950408889634


def wrap(v, n):
    return jnp.where(v >= n, v - n, v)


def kernel(li, lt, ri, rt, w, ki, ko, learn, grad, owner,
           img, txt, wv, kiv, kov, buf, hsrc, hall, lsrc, lall,
           chunks, rsbuf, red, zbuf, agbuf, ls, ss, rs, many):
    pairs, width = img.shape[1], img.shape[2]
    cols = w.shape[0]
    n_tower = N_ZL * N_X * N_C
    piece = pairs // n_tower
    split = 6 * width // 9
    scale = 1.0 / math.sqrt(width)
    d, t = lax.axis_index("dp"), lax.axis_index("tower")
    y = d // N_ZH
    zh = d - y * N_ZH
    zl = t // (N_X * N_C)
    xc = t - zl * (N_X * N_C)
    x = xc // N_C
    c = xc - x * N_C
    ys = [wrap(y + k, N_Y) for k in range(N_Y)]
    at_y = [(ys[k] * N_ZH + zh, t) for k in range(N_Y)]
    at_z = [(y * N_ZH + wrap(zh + k, N_ZH), t) for k in range(N_ZH)]
    at_t = []
    for k in (4, 3, 5, 2, 6, 1, 7, 0):
        xk = wrap(x + k, N_X)
        for dz in (1, 0):
            zk = 1 - zl if dz else zl
            for dc in (1, 0):
                if k or dz or dc:
                    tk = zk * (N_X * N_C) + xk * N_C + (1 - c if dc else c)
                    at_t.append(((d, tk), zk * 2 + jnp.where(xk >= N_X // 2, 1, 0)))

    peers = at_y[1:] + at_z[1:] + [p for p, _ in at_t]
    sent = []

    def send(src, dst, device):
        i = len(sent)
        copy = pltpu.make_async_remote_copy(
            src_ref=src, dst_ref=dst, send_sem=ss.at[i], recv_sem=rs.at[i],
            device_id=device, device_id_type=MESH)
        copy.start()
        sent.append(copy)
        return copy

    def to_tower(src_of, dst, sems):
        for p, tile in at_t:
            pltpu.make_async_remote_copy(
                src_ref=src_of(tile), dst_ref=dst, send_sem=many.at[sems], recv_sem=many.at[sems + 1],
                device_id=p, device_id_type=MESH).start()

    def wait_tower(ref, sem):
        other = ref.at[pl.ds(0, n_tower - 1)]
        pltpu.make_async_copy(other, other, many.at[sem]).wait()

    barrier = pltpu.get_barrier_semaphore()
    for p in peers:
        pl.semaphore_signal(barrier, inc=1, device_id=p, device_id_type=MESH)
    own = pl.ds(pl.multiple_of(t * piece, piece), piece)
    loads = [(lt.at[own], buf.at[0, 0, 0]), (rt.at[own], buf.at[1, 0, 0]),
             (li, img.at[0]), (w, wv), (lt, txt), (ki, kiv), (ko, kov), (ri, img.at[1])]
    loads = [pltpu.make_async_copy(a, b, ls.at[i]) for i, (a, b) in enumerate(loads)]
    for copy in loads:
        copy.start()
    pl.semaphore_wait(barrier, len(peers))

    low, high = pl.ds(0, split), pl.ds(split, width - split)
    full = pl.ds(0, width)
    texts = (lt, rt)
    z_in = {}
    for m in range(2):
        for k in (1, 3):
            z_in[m, k] = send(texts[m].at[own, low], buf.at[m, 0, ZPOS[N_ZH - k], :, low], at_z[k])

    class Ring:
        def __init__(self, places, lanes):
            self.places, self.lanes, self.copies = places, lanes, {}

        def at(self, m, r):
            return buf.at[m, POS[r % N_Y], self.places, :, self.lanes]

        def step(self, n, m, s, src=None):
            r = -s * n
            self.copies[n, m, s] = send(self.at(m, r) if src is None else src, self.at(m, r - s), at_y[s % N_Y])

        def start(self):
            for m in range(2):
                for s in (1, -1):
                    self.step(0, m, s)

        def relay(self, n):
            for m in range(2):
                for s in (1, -1):
                    if (n, m, s) in self.copies:
                        self.copies[n, m, s].wait_recv()
                        if n < 2 or (n == 2 and (s == 1) == (m == 0)):
                            self.step(n + 1, m, s)

    ring0 = Ring(0, full)
    ring1 = Ring(pl.ds(1, 2), low)
    ring2 = Ring(3, low)
    for m in range(2):
        for s in (1, -1):
            ring0.step(0, m, s, texts[m].at[own])

    def z_relay(copies, a, n, lanes):
        for m in range(2):
            for k in (1, 3):
                copies[m, k].wait_recv()
        for m, k in ((0, 1), (1, 3)):
            copies[m, 2] = send(buf.at[m, pl.ds(a, n), ZPOS[N_ZH - k], :, lanes],
                                buf.at[m, pl.ds(a, n), 3, :, lanes], at_z[k])

    def z_high(a, n):
        copies = {}
        for m in range(2):
            for k in (1, 3):
                copies[m, k] = send(buf.at[m, pl.ds(a, n), 0, :, high],
                                    buf.at[m, pl.ds(a, n), ZPOS[N_ZH - k], :, high], at_z[k])
        return copies

    for copy in loads[:5]:
        copy.wait()
    nt = (((1,), (1,)), ((), ()))

    def dot_nt(a, b):
        return lax.dot_general(a, b, nt, preferred_element_type=jnp.float32)

    pad = -(-cols // 8) * 8
    col = lax.broadcasted_iota(jnp.int32, (pad, width), 0)
    place = lax.broadcasted_iota(jnp.int32, (pad, width), 1)
    choose = jnp.where((place == t * cols + col) & (col < cols), 1.0, 0.0).astype(jnp.bfloat16)
    text_cols = dot_nt(choose, txt[...])
    projected = dot_nt(wv[...], img[0])
    part = jnp.sum(projected * text_cols[:cols], 0, keepdims=True)
    hsrc[...] = part
    hall[t] = part
    to_tower(lambda tile: hsrc, hall.at[t], 0)

    ring0.relay(0)
    high_a = z_high(0, 3)
    z_relay(z_in, 0, 1, low)
    ring1.start()
    ring0.relay(1)
    for m in range(2):
        z_in[m, 2].wait_recv()
    ring2.start()
    ring1.relay(0)
    ring0.relay(2)
    for copy in loads[5:]:
        copy.wait()
    z_relay(high_a, 0, 3, high)
    ring2.relay(0)
    ring1.relay(1)
    ring0.relay(3)
    high_b = z_high(3, N_Y - 3)

    lane = lax.broadcasted_iota(jnp.int32, (8, pairs), 1)
    sub = lax.broadcasted_iota(jnp.int32, (8, pairs), 0)

    def losses(m, start, count, with_own):
        text = buf[m, :, start:start + count].reshape(N_Y * count * piece, width)
        logits = dot_nt(text, img[m])
        linear = jnp.zeros((8, pairs), jnp.float32)
        prod = jnp.zeros((8, pairs), jnp.float32)
        logs = jnp.zeros((8, pairs), jnp.float32)
        diag = jnp.zeros((8, pairs), jnp.float32)
        groups = text.shape[0] // 8
        for g in range(groups):
            v = logits[8 * g:8 * g + 8]
            e = jnp.exp2(-jnp.abs(v * (scale * LOG2E)))
            lin = jnp.maximum(v * (scale / pairs), 0.0)
            if with_own and g < piece // 8:
                is_diag = lane == t * piece + 8 * g + sub
                diag = diag + jnp.where(is_diag, jnp.maximum(-v * scale, 0.0) + jnp.log1p(e), 0.0)
                e = jnp.where(is_diag, 0.0, e)
                lin = jnp.where(is_diag, 0.0, lin)
            linear = linear + lin
            prod = prod * (1.0 + e) + e
            if g % 16 == 15 or g == groups - 1:
                logs = logs + jnp.log1p(prod)
                prod = jnp.zeros((8, pairs), jnp.float32)
        return diag + linear + logs * (1.0 / pairs)

    def both(start, count, with_own=False):
        return losses(0, start, count, with_own) - losses(1, start, count, with_own)

    total = both(0, 1, True)

    wait_tower(hall, 1)
    head_logit = jnp.sum(hall[...], 0) * scale
    e = jnp.exp(-jnp.abs(head_logit))
    head_loss = jnp.maximum(-head_logit, 0.0) + jnp.log1p(e)
    slope = -(jnp.where(head_logit >= 0.0, e, 1.0) / (1.0 + e)) * scale
    kept = kiv.shape[1]
    hit = lax.broadcasted_iota(jnp.int32, (pairs, kept), 0) == kiv[...]
    hit = jnp.where(hit, 1.0, 0.0).astype(jnp.bfloat16)
    owner_plus = jnp.broadcast_to(kov[...].astype(jnp.float32) + 1.0, (16, kept)).astype(jnp.bfloat16)
    owner_of = dot_nt(owner_plus, hit)[:1]
    slope = jnp.where(owner_of > 0.5, slope, 0.0)
    slope_text = (text_cols * slope).astype(jnp.bfloat16)
    grad_part = jnp.dot(slope_text, img[0], preferred_element_type=jnp.float32)
    n_dp = N_Y * N_ZH
    each = lax.broadcasted_iota(jnp.int32, (n_dp, pairs), 0)
    mine = owner_of == (each + 1).astype(jnp.float32)
    owner_col = jnp.sum(jnp.where(mine, head_loss, 0.0), 1, keepdims=True)
    on_lane = lax.broadcasted_iota(jnp.int32, (n_dp, 128), 0) == lax.broadcasted_iota(jnp.int32, (n_dp, 128), 1)
    owner_row = jnp.sum(jnp.where(on_lane, owner_col, 0.0), 0, keepdims=True)
    wide = width // 128
    n_tiles = (pad // 8) * wide
    for i in range(N_Y * TILES):
        if i < n_tiles:
            a, b = 8 * (i // wide), 128 * (i % wide)
            tile = grad_part[a:a + 8, b:b + 128]
        elif i == n_tiles:
            tile = jnp.broadcast_to(owner_row, (8, 128))
        else:
            tile = jnp.zeros((8, 128), jnp.float32)
        chunks[i // TILES, i % TILES] = tile
    scattered = [send(chunks.at[ys[k]], rsbuf.at[k - 1], at_y[k]) for k in (4, 3, 5, 2, 6, 1, 7)]

    ring2.relay(1)
    ring1.relay(2)
    for m in range(2):
        high_a[m, 2].wait_recv()
    ring2.relay(2)
    z_relay(high_b, 3, N_Y - 3, high)

    for copy in scattered:
        copy.wait_recv()
    value = chunks[y]
    for k in range(N_Y - 1):
        value = value + rsbuf[k]
    red[...] = value
    zbuf[zh] = value
    summed = [send(red, zbuf.at[zh], at_z[k]) for k in (2, 1, 3)]

    ring1.relay(3)
    total = total + both(1, 2)

    for copy in summed:
        copy.wait_recv()
    value = zbuf[0]
    for k in range(1, N_ZH):
        value = value + zbuf[k]
    rest = value - value.astype(jnp.bfloat16).astype(jnp.float32)
    at = lax.broadcasted_iota(jnp.int32, value.shape, 0) * 8 + lax.broadcasted_iota(jnp.int32, value.shape, 1)
    low_half = (at >= 8 * (n_tiles % TILES) + 4) & (at < 8 * (n_tiles % TILES) + 8) & (y == n_tiles // TILES)
    value = jnp.where(low_half, rest, value)
    agbuf[y] = value.reshape(8 * TILES, 128).astype(jnp.bfloat16)
    gathered = [send(agbuf.at[y], agbuf.at[y], at_y[k]) for k in (4, 3, 5, 2, 6, 1, 7)]

    ring2.relay(3)
    for m in range(2):
        high_b[m, 2].wait_recv()
    total = total + both(3, 1)

    diff = jnp.sum(total, 0, keepdims=True)
    for i in range(pairs // 128):
        lsrc[i] = diff[:, 128 * i:128 * i + 128]
    own_tile = zl * 2 + jnp.where(x >= N_X // 2, 1, 0)
    lall[t] = lsrc[own_tile]
    to_tower(lambda tile: lsrc.at[tile], lall.at[t], 2)

    for copy in gathered:
        copy.wait_recv()
    for i in range(n_tiles):
        a, b = 8 * (i // wide), 128 * (i % wide)
        n, r = min(8, cols - a), 8 * (i % TILES)
        if i % 2 == 0:
            pair = agbuf[i // TILES, r:r + 16].astype(jnp.float32)
        grad[a:a + n, b:b + 128] = pair[8 * (i % 2):8 * (i % 2) + n]
    r = 8 * (n_tiles % TILES) // 16 * 16
    pair = agbuf[n_tiles // TILES, r:r + 16].astype(jnp.float32)
    pair = pair[8 * (n_tiles % 2):8 * (n_tiles % 2) + 8]
    all_owners = pair[:1] + pair[4:5]
    pick = lax.broadcasted_iota(jnp.int32, (1, 128), 1) == d
    owner[...] = jnp.broadcast_to(jnp.sum(jnp.where(pick, all_owners, 0.0), 1, keepdims=True), (1, 128))

    wait_tower(lall, 3)
    rows = jnp.broadcast_to(jnp.sum(lall[...], 0), (8, 128))
    first = (xc - jnp.where(x >= N_X // 2, N_X, 0)) * piece
    learn[...] = pltpu.roll(rows, jnp.where(first > 0, 128 - first, 0), 1)[:1]
    wait_tower(hall, 0)
    wait_tower(lall, 2)
    for copy in sent:
        copy.wait_send()


def local(learner_image, learner_text, ref_image, ref_text, head_weight, kept_index, kept_owner):
    pairs, width = learner_image.shape
    cols = head_weight.shape[0]
    kept = kept_index.shape[0]
    f32, bf16, i32 = jnp.float32, jnp.bfloat16, jnp.int32
    any_space = pl.BlockSpec(memory_space=pl.ANY)
    vmem = pl.BlockSpec(memory_space=pltpu.VMEM)
    learn, grad, owner = pl.pallas_call(
        kernel,
        out_shape=(
            jax.ShapeDtypeStruct((1, 128), f32),
            jax.ShapeDtypeStruct((cols, width), f32),
            jax.ShapeDtypeStruct((1, 128), f32),
        ),
        in_specs=[any_space] * 7,
        out_specs=(vmem, vmem, vmem),
        scratch_shapes=[
            pltpu.VMEM((2, pairs, width), bf16),
            pltpu.VMEM((pairs, width), bf16),
            pltpu.VMEM((cols, width), bf16),
            pltpu.VMEM((1, kept), i32),
            pltpu.VMEM((1, kept), i32),
            pltpu.VMEM((2, N_Y, N_ZH, pairs // 32, width), bf16),
            pltpu.VMEM((1, pairs), f32),
            pltpu.VMEM((32, 1, pairs), f32),
            pltpu.VMEM((4, 1, 128), f32),
            pltpu.VMEM((32, 1, 128), f32),
            pltpu.VMEM((N_Y, TILES, 8, 128), f32),
            pltpu.VMEM((N_Y - 1, TILES, 8, 128), f32),
            pltpu.VMEM((TILES, 8, 128), f32),
            pltpu.VMEM((N_ZH, TILES, 8, 128), f32),
            pltpu.VMEM((N_Y, 8 * TILES, 128), bf16),
            pltpu.SemaphoreType.DMA((8,)),
            pltpu.SemaphoreType.DMA((96,)),
            pltpu.SemaphoreType.DMA((96,)),
            pltpu.SemaphoreType.DMA((4,)),
        ],
        compiler_params=pltpu.CompilerParams(
            collective_id=0, has_side_effects=True, vmem_limit_bytes=62 * 1024 * 1024
        ),
    )(
        learner_image,
        learner_text,
        ref_image,
        ref_text,
        head_weight,
        kept_index.reshape(1, kept),
        kept_owner.reshape(1, kept),
    )
    return learn[0, : pairs // 32], grad, owner[0, :1]


def solution(mesh):
    placed = (
        P("dp", None),
        P("dp", None),
        P("dp", None),
        P("dp", None),
        P("tower", None),
        P("dp"),
        P("dp", None),
    )
    return jax.shard_map(
        local,
        mesh=mesh,
        in_specs=placed,
        out_specs=(P(("dp", "tower")), P("tower", None), P("dp")),
        check_vma=False,
    )
```

```python
import math

import jax
import jax.numpy as jnp
from jax import lax
from jax.experimental import pallas as pl
from jax.experimental.pallas import tpu as pltpu
from jax.sharding import PartitionSpec as P

MESH = pl.DeviceIdType.MESH
N_Y, N_ZH, N_ZL, N_X, N_C = 8, 4, 2, 8, 2
POS = (0, 2, 4, 6, 7, 5, 3, 1)
ZPOS = (0, 1, 3, 2)
TILES = 6
LOG2E = 1.4426950408889634


def wrap(v, n):
    return jnp.where(v >= n, v - n, v)


def kernel(li, lt, ri, rt, w, ki, ko, learn, grad, owner,
           img, txt, wv, kiv, kov, buf, hsrc, hall, lsrc, lall,
           chunks, rsbuf, red, zbuf, agbuf, ls, ss, rs, many):
    pairs, width = img.shape[1], img.shape[2]
    cols = w.shape[0]
    n_tower = N_ZL * N_X * N_C
    piece = pairs // n_tower
    split = 6 * width // 9
    scale = 1.0 / math.sqrt(width)
    d, t = lax.axis_index("dp"), lax.axis_index("tower")
    y = d // N_ZH
    zh = d - y * N_ZH
    zl = t // (N_X * N_C)
    xc = t - zl * (N_X * N_C)
    x = xc // N_C
    c = xc - x * N_C
    ys = [wrap(y + k, N_Y) for k in range(N_Y)]
    at_y = [(ys[k] * N_ZH + zh, t) for k in range(N_Y)]
    at_z = [(y * N_ZH + wrap(zh + k, N_ZH), t) for k in range(N_ZH)]
    at_t = []
    for k in (4, 3, 5, 2, 6, 1, 7, 0):
        xk = wrap(x + k, N_X)
        for dz in (1, 0):
            zk = 1 - zl if dz else zl
            for dc in (1, 0):
                if k or dz or dc:
                    tk = zk * (N_X * N_C) + xk * N_C + (1 - c if dc else c)
                    at_t.append(((d, tk), zk * 2 + jnp.where(xk >= N_X // 2, 1, 0)))

    peers = at_y[1:] + at_z[1:] + [p for p, _ in at_t]
    sent = []

    def send(src, dst, device):
        i = len(sent)
        copy = pltpu.make_async_remote_copy(
            src_ref=src, dst_ref=dst, send_sem=ss.at[i], recv_sem=rs.at[i],
            device_id=device, device_id_type=MESH)
        copy.start()
        sent.append(copy)
        return copy

    def to_tower(src_of, dst, sems):
        for p, tile in at_t:
            pltpu.make_async_remote_copy(
                src_ref=src_of(tile), dst_ref=dst, send_sem=many.at[sems], recv_sem=many.at[sems + 1],
                device_id=p, device_id_type=MESH).start()

    def wait_tower(ref, sem):
        other = ref.at[pl.ds(0, n_tower - 1)]
        pltpu.make_async_copy(other, other, many.at[sem]).wait()

    own = pl.ds(pl.multiple_of(t * piece, piece), piece)
    loads = [(lt.at[own], buf.at[0, 0, 0]), (rt.at[own], buf.at[1, 0, 0]),
             (li, img.at[0]), (w, wv), (lt, txt), (ki, kiv), (ko, kov), (ri, img.at[1])]
    loads = [pltpu.make_async_copy(a, b, ls.at[i]) for i, (a, b) in enumerate(loads)]
    for copy in loads:
        copy.start()
    barrier = pltpu.get_barrier_semaphore()
    for p in peers:
        pl.semaphore_signal(barrier, inc=1, device_id=p, device_id_type=MESH)
    loads[0].wait()
    loads[1].wait()
    pl.semaphore_wait(barrier, len(peers))

    low, high = pl.ds(0, split), pl.ds(split, width - split)
    full = pl.ds(0, width)
    z_in = {}
    for k in (1, 3):
        z_in[k] = send(buf.at[:, 0, 0, :, low], buf.at[:, 0, ZPOS[N_ZH - k], :, low], at_z[k])

    class Ring:
        def __init__(self, places, lanes):
            self.places, self.lanes, self.copies = places, lanes, {}

        def at(self, m, r):
            return buf.at[m, POS[r % N_Y], self.places, :, self.lanes]

        def step(self, n, s):
            r = -s * n
            m = slice(None) if n < 3 else (0 if s == 1 else 1)
            self.copies[n, s] = send(self.at(m, r), self.at(m, r - s), at_y[s % N_Y])

        def start(self):
            for s in (1, -1):
                self.step(0, s)

        def relay(self, n):
            for s in (1, -1):
                self.copies[n, s].wait_recv()
                if n < 3:
                    self.step(n + 1, s)

    ring0 = Ring(0, full)
    ring1 = Ring(pl.ds(1, 2), low)
    ring2 = Ring(3, low)
    ring0.start()

    def z_relay(copies, a, n, lanes):
        for k in (1, 3):
            copies[k].wait_recv()
        for m, k in ((0, 1), (1, 3)):
            copies[m, 2] = send(buf.at[m, pl.ds(a, n), ZPOS[N_ZH - k], :, lanes],
                                buf.at[m, pl.ds(a, n), 3, :, lanes], at_z[k])

    def z_high(a, n):
        copies = {}
        for k in (1, 3):
            copies[k] = send(buf.at[:, pl.ds(a, n), 0, :, high],
                             buf.at[:, pl.ds(a, n), ZPOS[N_ZH - k], :, high], at_z[k])
        return copies

    for copy in loads[2:5]:
        copy.wait()
    nt = (((1,), (1,)), ((), ()))

    def dot_nt(a, b):
        return lax.dot_general(a, b, nt, preferred_element_type=jnp.float32)

    pad = -(-cols // 8) * 8
    col = lax.broadcasted_iota(jnp.int32, (pad, width), 0)
    place = lax.broadcasted_iota(jnp.int32, (pad, width), 1)
    choose = jnp.where((place == t * cols + col) & (col < cols), 1.0, 0.0).astype(jnp.bfloat16)
    text_cols = dot_nt(choose, txt[...])
    projected = dot_nt(wv[...], img[0])
    part = jnp.sum(projected * text_cols[:cols], 0, keepdims=True)
    hsrc[...] = part
    hall[t] = part
    to_tower(lambda tile: hsrc, hall.at[t], 0)

    ring0.relay(0)
    high_a = z_high(0, 3)
    z_relay(z_in, 0, 1, low)
    ring1.start()
    ring0.relay(1)
    for m in range(2):
        z_in[m, 2].wait_recv()
    ring2.start()
    ring1.relay(0)
    ring0.relay(2)
    for copy in loads[5:]:
        copy.wait()
    z_relay(high_a, 0, 3, high)
    ring2.relay(0)
    ring1.relay(1)
    ring0.relay(3)
    high_b = z_high(3, N_Y - 3)

    lane = lax.broadcasted_iota(jnp.int32, (8, pairs), 1)
    sub = lax.broadcasted_iota(jnp.int32, (8, pairs), 0)

    def losses(m, start, count, with_own):
        text = buf[m, :, start:start + count].reshape(N_Y * count * piece, width)
        logits = dot_nt(text, img[m])
        linear = jnp.zeros((8, pairs), jnp.float32)
        prod = jnp.zeros((8, pairs), jnp.float32)
        logs = jnp.zeros((8, pairs), jnp.float32)
        diag = jnp.zeros((8, pairs), jnp.float32)
        groups = text.shape[0] // 8
        for g in range(groups):
            v = logits[8 * g:8 * g + 8]
            e = jnp.exp2(-jnp.abs(v * (scale * LOG2E)))
            lin = jnp.maximum(v * (scale / pairs), 0.0)
            if with_own and g < piece // 8:
                is_diag = lane == t * piece + 8 * g + sub
                diag = diag + jnp.where(is_diag, jnp.maximum(-v * scale, 0.0) + jnp.log1p(e), 0.0)
                e = jnp.where(is_diag, 0.0, e)
                lin = jnp.where(is_diag, 0.0, lin)
            linear = linear + lin
            prod = prod * (1.0 + e) + e
            if g % 16 == 15 or g == groups - 1:
                logs = logs + jnp.log1p(prod)
                prod = jnp.zeros((8, pairs), jnp.float32)
        return diag + linear + logs * (1.0 / pairs)

    def both(start, count, with_own=False):
        return losses(0, start, count, with_own) - losses(1, start, count, with_own)

    total = both(0, 1, True)

    wait_tower(hall, 1)
    head_logit = jnp.sum(hall[...], 0) * scale
    e = jnp.exp(-jnp.abs(head_logit))
    head_loss = jnp.maximum(-head_logit, 0.0) + jnp.log1p(e)
    slope = -(jnp.where(head_logit >= 0.0, e, 1.0) / (1.0 + e)) * scale
    kept = kiv.shape[1]
    hit = lax.broadcasted_iota(jnp.int32, (pairs, kept), 0) == kiv[...]
    hit = jnp.where(hit, 1.0, 0.0).astype(jnp.bfloat16)
    owner_plus = jnp.broadcast_to(kov[...].astype(jnp.float32) + 1.0, (16, kept)).astype(jnp.bfloat16)
    owner_of = dot_nt(owner_plus, hit)[:1]
    slope = jnp.where(owner_of > 0.5, slope, 0.0)
    slope_text = (text_cols * slope).astype(jnp.bfloat16)
    grad_part = jnp.dot(slope_text, img[0], preferred_element_type=jnp.float32)
    n_dp = N_Y * N_ZH
    each = lax.broadcasted_iota(jnp.int32, (n_dp, pairs), 0)
    mine = owner_of == (each + 1).astype(jnp.float32)
    owner_col = jnp.sum(jnp.where(mine, head_loss, 0.0), 1, keepdims=True)
    on_lane = lax.broadcasted_iota(jnp.int32, (n_dp, 128), 0) == lax.broadcasted_iota(jnp.int32, (n_dp, 128), 1)
    owner_row = jnp.sum(jnp.where(on_lane, owner_col, 0.0), 0, keepdims=True)
    wide = width // 128
    n_tiles = (pad // 8) * wide
    for i in range(N_Y * TILES):
        if i < n_tiles:
            a, b = 8 * (i // wide), 128 * (i % wide)
            tile = grad_part[a:a + 8, b:b + 128]
        elif i == n_tiles:
            tile = jnp.broadcast_to(owner_row, (8, 128))
        else:
            tile = jnp.zeros((8, 128), jnp.float32)
        chunks[i // TILES, i % TILES] = tile
    scattered = [send(chunks.at[ys[k]], rsbuf.at[k - 1], at_y[k]) for k in (4, 3, 5, 2, 6, 1, 7)]

    ring2.relay(1)
    ring1.relay(2)
    z_relay(high_b, 3, N_Y - 3, high)
    ring2.relay(2)
    for m in range(2):
        high_a[m, 2].wait_recv()

    for copy in scattered:
        copy.wait_recv()
    value = chunks[y]
    for k in range(N_Y - 1):
        value = value + rsbuf[k]
    red[...] = value
    zbuf[zh] = value
    summed = [send(red, zbuf.at[zh], at_z[k]) for k in (2, 1, 3)]

    ring1.relay(3)
    total = total + both(1, 2)

    for copy in summed:
        copy.wait_recv()
    value = zbuf[0]
    for k in range(1, N_ZH):
        value = value + zbuf[k]
    rest = value - value.astype(jnp.bfloat16).astype(jnp.float32)
    at = lax.broadcasted_iota(jnp.int32, value.shape, 0) * 8 + lax.broadcasted_iota(jnp.int32, value.shape, 1)
    low_half = (at >= 8 * (n_tiles % TILES) + 4) & (at < 8 * (n_tiles % TILES) + 8) & (y == n_tiles // TILES)
    value = jnp.where(low_half, rest, value)
    agbuf[y] = value.reshape(8 * TILES, 128).astype(jnp.bfloat16)
    gathered = [send(agbuf.at[y], agbuf.at[y], at_y[k]) for k in (4, 3, 5, 2, 6, 1, 7)]

    ring2.relay(3)
    for m in range(2):
        high_b[m, 2].wait_recv()
    total = total + both(3, 1)

    diff = jnp.sum(total, 0, keepdims=True)
    for i in range(pairs // 128):
        lsrc[i] = diff[:, 128 * i:128 * i + 128]
    own_tile = zl * 2 + jnp.where(x >= N_X // 2, 1, 0)
    lall[t] = lsrc[own_tile]
    to_tower(lambda tile: lsrc.at[tile], lall.at[t], 2)

    for copy in gathered:
        copy.wait_recv()
    for i in range(n_tiles):
        a, b = 8 * (i // wide), 128 * (i % wide)
        n, r = min(8, cols - a), 8 * (i % TILES)
        if i % 2 == 0:
            pair = agbuf[i // TILES, r:r + 16].astype(jnp.float32)
        grad[a:a + n, b:b + 128] = pair[8 * (i % 2):8 * (i % 2) + n]
    r = 8 * (n_tiles % TILES) // 16 * 16
    pair = agbuf[n_tiles // TILES, r:r + 16].astype(jnp.float32)
    pair = pair[8 * (n_tiles % 2):8 * (n_tiles % 2) + 8]
    all_owners = pair[:1] + pair[4:5]
    pick = lax.broadcasted_iota(jnp.int32, (1, 128), 1) == d
    owner[...] = jnp.broadcast_to(jnp.sum(jnp.where(pick, all_owners, 0.0), 1, keepdims=True), (1, 128))

    wait_tower(lall, 3)
    rows = jnp.broadcast_to(jnp.sum(lall[...], 0), (8, 128))
    first = (xc - jnp.where(x >= N_X // 2, N_X, 0)) * piece
    learn[...] = pltpu.roll(rows, jnp.where(first > 0, 128 - first, 0), 1)[:1]
    wait_tower(hall, 0)
    wait_tower(lall, 2)
    for copy in sent:
        copy.wait_send()


def local(learner_image, learner_text, ref_image, ref_text, head_weight, kept_index, kept_owner):
    pairs, width = learner_image.shape
    cols = head_weight.shape[0]
    kept = kept_index.shape[0]
    f32, bf16, i32 = jnp.float32, jnp.bfloat16, jnp.int32
    any_space = pl.BlockSpec(memory_space=pl.ANY)
    vmem = pl.BlockSpec(memory_space=pltpu.VMEM)
    learn, grad, owner = pl.pallas_call(
        kernel,
        out_shape=(
            jax.ShapeDtypeStruct((1, 128), f32),
            jax.ShapeDtypeStruct((cols, width), f32),
            jax.ShapeDtypeStruct((1, 128), f32),
        ),
        in_specs=[any_space] * 7,
        out_specs=(vmem, vmem, vmem),
        scratch_shapes=[
            pltpu.VMEM((2, pairs, width), bf16),
            pltpu.VMEM((pairs, width), bf16),
            pltpu.VMEM((cols, width), bf16),
            pltpu.VMEM((1, kept), i32),
            pltpu.VMEM((1, kept), i32),
            pltpu.VMEM((2, N_Y, N_ZH, pairs // 32, width), bf16),
            pltpu.VMEM((1, pairs), f32),
            pltpu.VMEM((32, 1, pairs), f32),
            pltpu.VMEM((4, 1, 128), f32),
            pltpu.VMEM((32, 1, 128), f32),
            pltpu.VMEM((N_Y, TILES, 8, 128), f32),
            pltpu.VMEM((N_Y - 1, TILES, 8, 128), f32),
            pltpu.VMEM((TILES, 8, 128), f32),
            pltpu.VMEM((N_ZH, TILES, 8, 128), f32),
            pltpu.VMEM((N_Y, 8 * TILES, 128), bf16),
            pltpu.SemaphoreType.DMA((8,)),
            pltpu.SemaphoreType.DMA((96,)),
            pltpu.SemaphoreType.DMA((96,)),
            pltpu.SemaphoreType.DMA((4,)),
        ],
        compiler_params=pltpu.CompilerParams(
            collective_id=0, has_side_effects=True, vmem_limit_bytes=62 * 1024 * 1024
        ),
    )(
        learner_image,
        learner_text,
        ref_image,
        ref_text,
        head_weight,
        kept_index.reshape(1, kept),
        kept_owner.reshape(1, kept),
    )
    return learn[0, : pairs // 32], grad, owner[0, :1]


def solution(mesh):
    placed = (
        P("dp", None),
        P("dp", None),
        P("dp", None),
        P("dp", None),
        P("tower", None),
        P("dp"),
        P("dp", None),
    )
    return jax.shard_map(
        local,
        mesh=mesh,
        in_specs=placed,
        out_specs=(P(("dp", "tower")), P("tower", None), P("dp")),
        check_vma=False,
    )
```
